32 devices in a mesh: dp: 16 (over z, x, core), tensor: 2 (over y).
Axes of the slice: x: 2, y: 2, z: 4, core: 2. Of those that a mesh axis runs over, the one named last changes fastest.
Arguments:
- tokens: bfloat16 [16384, 1024], P(('dp', 'tensor')), may hold values from -6 to 6
- slot_seq: int32 [16384], P('dp'), may hold values from 0 to 7, as said below
- seq_len: int32 [128], P('dp'), may hold values from 0 to 1024, as said below
- ln1_gain: bfloat16 [1024], P('dp'), may hold values from 0.5 to 1.5
- ln1_shift: bfloat16 [1024], P('dp'), may hold values from -3 to 3
- qkv_weight: bfloat16 [1024, 3, 1024], P('dp', None, 'tensor'), may hold values from -0.1875 to 0.1875
- qkv_bias: bfloat16 [2, 16, 64], P(None, 'tensor', 'dp'), may hold values from -3 to 3
- out_weight: bfloat16 [1024, 1024], P('tensor', 'dp'), may hold values from -0.75 to 0.75
- out_bias: bfloat16 [1024], P('dp'), may hold values from -3 to 3
- ln2_gain: bfloat16 [1024], P('dp'), may hold values from 0.5 to 1.5
- ln2_shift: bfloat16 [1024], P('dp'), may hold values from -3 to 3
- up_weight: bfloat16 [1024, 4096], P('dp', 'tensor'), may hold values from -0.1875 to 0.1875
- up_bias: bfloat16 [64, 64], P('tensor', 'dp'), may hold values from -3 to 3
- down_weight: bfloat16 [4096, 1024], P('tensor', 'dp'), may hold values from -0.09375 to 0.09375
- down_bias: bfloat16 [1024], P('dp'), may hold values from -3 to 3
- cotangent: bfloat16 [16384, 1024], P(('dp', 'tensor')), may hold values from -6 to 6
Outputs:
- output: float32 [16384, 1024], P(('dp', 'tensor'))
- grad_tokens: float32 [16384, 1024], P(('dp', 'tensor'))
- grad_ln1_gain: float32 [1024], P('dp')
- grad_ln1_shift: float32 [1024], P('dp')
- grad_qkv_weight: float32 [1024, 3, 1024], P('dp', None, 'tensor')
- grad_qkv_bias: float32 [2, 16, 64], P(None, 'tensor', 'dp')
- grad_out_weight: float32 [1024, 1024], P('tensor', 'dp')
- grad_out_bias: float32 [1024], P('dp')
- grad_ln2_gain: float32 [1024], P('dp')
- grad_ln2_shift: float32 [1024], P('dp')
- grad_up_weight: float32 [1024, 4096], P('dp', 'tensor')
- grad_up_bias: float32 [64, 64], P('tensor', 'dp')
- grad_down_weight: float32 [4096, 1024], P('tensor', 'dp')
- grad_down_bias: float32 [1024], P('dp')
The draws below stay inside these ranges and needn't reach their ends.
Inputs may be any that keep to these rules, and one draw needn't show every extreme that they name: Within each group of 1024 slots, slot_seq starts at 0, never falls, rises by one at a time and changes only at multiples of 128; a sequence's live tokens are its first slots; some group holds 8 sequences of one block each. `seq_len`: A length is 0 exactly for sequence numbers that mark empty blocks or are unused; a live sequence fits its blocks and has at least one live token; some group holds one sequence of 1024 live tokens.
All inputs are finite; a program needn't handle non-finite values.
Results may differ from the reference program's by a relative error of at most 0.02.
Values may be sent and summed in bfloat16 or wider, within the bound.
A program may use at most 192 MiB of HBM per device.

```python
import jax
import jax.numpy as jnp
from jax import lax

D = 1024
H = 16
HD = 64
FF = 4096
CAP = 1024
BLOCK = 128
TOKENS = 16384
N_TENSOR = 2


def layout_draw(key):
    group_list = TOKENS // CAP
    block_list = CAP // BLOCK
    draw_keys = jax.random.split(jax.random.fold_in(key, 7), 5)
    block_position = jnp.arange(block_list, dtype=jnp.int32)
    group_index = jnp.arange(group_list, dtype=jnp.int32)
    starts = jax.random.randint(draw_keys[0], (group_list, block_list), 0, 3) == 0
    starts = starts | (block_position[None, :] == 0)
    full_group = jax.random.randint(draw_keys[1], (), 0, group_list)
    busy_group = (full_group + 1 + jax.random.randint(draw_keys[4], (), 0, group_list - 1)) % group_list
    group_complete = group_index == full_group
    group_occupied = group_index == busy_group
    starts = jnp.where(group_complete[:, None], block_position[None, :] == 0, starts)
    starts = jnp.where(group_occupied[:, None], True, starts)
    empty_slots = jax.random.randint(draw_keys[2], (group_list,), 0, block_list // 2 + 1)
    empty_slots = jnp.where(group_complete | group_occupied, 0, empty_slots)
    used_slots = block_position[None, :] < (block_list - empty_slots)[:, None]
    seq_of_block = jnp.cumsum(starts.astype(jnp.int32), axis=1) - 1
    seq_count = jnp.sum((starts & used_slots).astype(jnp.int32), axis=1)
    seq_of_block = jnp.where(used_slots, seq_of_block, seq_count[:, None])
    member = (seq_of_block[:, :, None] == block_position[None, None, :]) & used_slots[:, :, None]
    block_count = jnp.sum(member.astype(jnp.int32), axis=1)
    last_fill = jax.random.randint(draw_keys[3], (group_list, block_list), 1, BLOCK + 1)
    last_fill = jnp.where(group_complete[:, None], BLOCK, last_fill)
    lengths = jnp.where(block_count > 0, BLOCK * (block_count - 1) + last_fill, 0)
    slots = jnp.repeat(seq_of_block, BLOCK, axis=1).reshape(TOKENS)
    return (slots.astype(jnp.int32), lengths.reshape(group_list * block_list).astype(jnp.int32))


def draw_slot_seq(key, part):
    return layout_draw(key)[0]


def draw_seq_len(key, part):
    return layout_draw(key)[1]


def block_levels(own_key, dims, cuts, smallest, top_value):
    factor_of, own = 1.0, jax.random.fold_in(own_key, 6)
    for axis_at, shards_of in cuts:
        draws = jnp.exp(jax.random.uniform(jax.random.fold_in(own, axis_at), (shards_of,), jnp.float32, smallest / len(cuts), top_value / len(cuts)))
        factor_of = factor_of * jnp.repeat(draws, dims[axis_at] // shards_of).reshape([-1 if axis == axis_at else 1 for axis in range(len(dims))])
    return factor_of


def noise(own_key, shape, scale, reach, cuts=(), held_as=jnp.bfloat16):
    drawn = jax.random.normal(own_key, shape, jnp.float32) * scale
    if len(cuts) > 0:
        drawn = block_levels(own_key, shape, cuts, -0.22, 0.18) * drawn
    return jnp.clip(drawn, min=-reach, max=reach).astype(held_as)


def setup_inputs(seed: int = 0) -> dict:
    splits = jax.random.split(jax.random.key(seed), 17)
    return {
        "tokens": noise(splits[0], (TOKENS, D), 1.0, 6.0, ((0, 32),)),
        "slot_seq": draw_slot_seq(jax.random.fold_in(splits[16], 71), 0),
        "seq_len": draw_seq_len(jax.random.fold_in(splits[16], 71), 0),
        "ln1_gain": jnp.clip(1.0 + 0.1 * jax.random.normal(splits[3], (D,), jnp.float32), 0.5, 1.5).astype(jnp.bfloat16),
        "ln1_shift": noise(splits[4], (D,), 0.3, 3.0, ((0, 16),)),
        "qkv_weight": noise(splits[5], (D, 3, D), D ** -0.5, 0.1875, ((0, 16), (2, 2))),
        "qkv_bias": noise(splits[6], (2, H, HD), 0.5, 3.0, ((1, 2), (2, 16))),
        "out_weight": noise(splits[7], (D, D), (D // 16) ** -0.5, 0.75, ((0, 2), (1, 16))),
        "out_bias": noise(splits[8], (D,), 0.5, 3.0, ((0, 16),)),
        "ln2_gain": jnp.clip(1.0 + 0.1 * jax.random.normal(splits[9], (D,), jnp.float32), 0.5, 1.5).astype(jnp.bfloat16),
        "ln2_shift": noise(splits[10], (D,), 0.3, 3.0, ((0, 16),)),
        "up_weight": noise(splits[11], (D, FF), D ** -0.5, 0.1875, ((0, 16), (1, 2))),
        "up_bias": noise(splits[12], (FF // HD, HD), 0.5, 3.0, ((0, 2), (1, 16))),
        "down_weight": noise(splits[13], (FF, D), FF ** -0.5, 0.09375, ((0, 2), (1, 16))),
        "down_bias": noise(splits[14], (D,), 0.5, 3.0, ((0, 16),)),
        "cotangent": noise(splits[15], (TOKENS, D), 1.0, 6.0, ((0, 32),)),
    }


epsilon = 1e-05
masked_fill = -1e+30
gelu_root = 0.7978845608028654
gelu_cubic = 0.044715

def layer_norm(hidden, gain, shift):
    center = hidden - lax.optimization_barrier(jnp.mean(hidden, axis=-1, keepdims=True))
    inverse = lax.rsqrt(lax.optimization_barrier(jnp.mean(center * center, axis=-1, keepdims=True)) + epsilon)
    normed = center * inverse
    return (normed * gain + shift, normed, inverse)

def norm_back(upstream, gain, normed, inverse):
    scaled = upstream * gain
    return inverse * (scaled - lax.optimization_barrier(jnp.mean(scaled, axis=-1, keepdims=True)) - normed * lax.optimization_barrier(jnp.mean(scaled * normed, axis=-1, keepdims=True)))

def gelu_value(inputs):
    tangent = jnp.tanh(gelu_root * (inputs + gelu_cubic * inputs * inputs * inputs))
    return 0.5 * inputs * (1.0 + tangent)

def gelu_slope(inputs):
    tangent = jnp.tanh(gelu_root * (inputs + gelu_cubic * inputs * inputs * inputs))
    return 0.5 * (1.0 + tangent) + 0.5 * inputs * (1.0 - tangent * tangent) * gelu_root * (1.0 + 3.0 * gelu_cubic * inputs * inputs)

def live_slots(slot_seq, seq_len):
    numbers = seq_len.shape[0]
    onehot = (slot_seq[:, None] == jnp.arange(numbers, dtype=jnp.int32)[None, :]).astype(jnp.int32)
    counts = lax.optimization_barrier(jnp.sum(onehot, axis=0, dtype=jnp.int32))
    first_slot = (jnp.cumsum(counts, dtype=jnp.int32) - counts).astype(jnp.int32)
    run_start = lax.optimization_barrier(jnp.sum(onehot * first_slot[None, :], axis=1, dtype=jnp.int32))
    run_length = lax.optimization_barrier(jnp.sum(onehot * seq_len[None, :], axis=1, dtype=jnp.int32))
    places = jnp.arange(slot_seq.shape[0], dtype=jnp.int32) - run_start
    return places < run_length

def grouped_product(left, right):
    width = left.shape[1] // N_TENSOR
    parts = jnp.einsum('tgk,gkd->gtd', left.reshape(left.shape[0], N_TENSOR, width).astype(jnp.float32), right.reshape(N_TENSOR, width, right.shape[1]).astype(jnp.float32))
    return lax.optimization_barrier(jnp.sum(parts.astype(jnp.bfloat16).astype(jnp.float32), axis=0))

def group_pass(params, tokens, cotangent, slot_seq, seq_len):
    ln1_gain, ln1_shift, qkv_weight, qkv_bias, out_weight, out_bias, ln2_gain, ln2_shift, up_weight, up_bias, down_weight, down_bias = params
    f32 = jnp.float32
    bf16 = jnp.bfloat16
    slots = tokens.shape[0]
    live = live_slots(slot_seq, seq_len)
    index = jnp.arange(slots, dtype=jnp.int32)
    allowed = (slot_seq[:, None] == slot_seq[None, :]) & (index[None, :] <= index[:, None]) & live[None, :]
    scale = HD ** (-0.5)
    inputs = tokens.astype(f32)
    a1_full, n1, r1 = layer_norm(inputs, ln1_gain.astype(f32), ln1_shift.astype(f32))
    a1 = a1_full.astype(bf16)
    qkv_full = jnp.einsum('td,dck->tck', a1.astype(f32), qkv_weight.astype(f32))
    bias_rows = qkv_bias.reshape(2, D).astype(f32)
    bias_all = jnp.stack([bias_rows[0], jnp.zeros((D,), f32), bias_rows[1]], axis=0)
    qkv = (qkv_full + bias_all[None]).astype(bf16)
    queries = qkv[:, 0].reshape(slots, H, HD).astype(f32)
    key_rows = qkv[:, 1].reshape(slots, H, HD).astype(f32)
    values = qkv[:, 2].reshape(slots, H, HD).astype(f32)
    scores = jnp.einsum('qhd,khd->hqk', queries, key_rows) * scale
    scores = jnp.where(allowed[None], scores, masked_fill)
    top = lax.optimization_barrier(jnp.max(scores, axis=-1, keepdims=True))
    lse = top + jnp.log(lax.optimization_barrier(jnp.sum(jnp.exp(scores - top), axis=-1, keepdims=True)))
    probs_full = jnp.exp(scores - lse)
    probs = probs_full.astype(bf16)
    heads = jnp.einsum('hqk,khd->qhd', probs.astype(f32), values).astype(bf16)
    heads_flat = heads.reshape(slots, D)
    attn = grouped_product(heads_flat, out_weight)
    h1 = inputs + attn + out_bias.astype(f32)
    a2_full, n2, r2 = layer_norm(h1, ln2_gain.astype(f32), ln2_shift.astype(f32))
    a2 = a2_full.astype(bf16)
    pre = jnp.dot(a2, up_weight, preferred_element_type=f32) + up_bias.reshape(FF).astype(f32)
    act = gelu_value(pre).astype(bf16)
    mlp = grouped_product(act, down_weight)
    output = jnp.where(live[:, None], h1 + mlp + down_bias.astype(f32), 0.0)
    grad_h2 = jnp.where(live[:, None], cotangent.astype(f32), 0.0)
    grad_h2_b = grad_h2.astype(bf16)
    grad_down_bias = lax.optimization_barrier(jnp.sum(grad_h2, axis=0))
    grad_down_weight = jnp.dot(act.T, grad_h2_b, preferred_element_type=f32)
    grad_pre = jnp.dot(grad_h2_b, down_weight.T, preferred_element_type=f32) * gelu_slope(pre)
    grad_up_bias = lax.optimization_barrier(jnp.sum(grad_pre, axis=0)).reshape(FF // HD, HD)
    grad_pre_b = grad_pre.astype(bf16)
    grad_up_weight = jnp.dot(a2.T, grad_pre_b, preferred_element_type=f32)
    grad_a2 = grouped_product(grad_pre_b, up_weight.T)
    grad_ln2_gain = lax.optimization_barrier(jnp.sum(grad_a2 * n2, axis=0))
    grad_ln2_shift = lax.optimization_barrier(jnp.sum(grad_a2, axis=0))
    grad_h1 = grad_h2 + norm_back(grad_a2, ln2_gain.astype(f32), n2, r2)
    grad_out_bias = lax.optimization_barrier(jnp.sum(grad_h1, axis=0))
    grad_h1_b = grad_h1.astype(bf16)
    grad_out_weight = jnp.dot(heads_flat.T, grad_h1_b, preferred_element_type=f32)
    grad_heads = jnp.dot(grad_h1_b, out_weight.T, preferred_element_type=f32).astype(bf16).reshape(slots, H, HD).astype(f32)
    delta = lax.optimization_barrier(jnp.sum(grad_heads * heads.astype(f32), axis=-1)).T
    grad_probs = jnp.einsum('qhd,khd->hqk', grad_heads, values)
    grad_scores = (probs_full * (grad_probs - delta[:, :, None]) * scale).astype(bf16).astype(f32)
    grad_q = jnp.einsum('hqk,khd->qhd', grad_scores, key_rows)
    grad_k = jnp.einsum('hqk,qhd->khd', grad_scores, queries)
    grad_v = jnp.einsum('hqk,qhd->khd', probs.astype(f32), grad_heads)
    grad_qkv_full = jnp.stack([grad_q, grad_k, grad_v], axis=1).reshape(slots, 3, D)
    grad_qkv_bias = jnp.stack([lax.optimization_barrier(jnp.sum(grad_q, axis=0)), lax.optimization_barrier(jnp.sum(grad_v, axis=0))], axis=0)
    grad_qkv = grad_qkv_full.astype(bf16)
    grad_qkv_weight = jnp.einsum('td,tck->dck', a1.astype(f32), grad_qkv.astype(f32))
    width = D // N_TENSOR
    parts = jnp.einsum('tcgk,dcgk->gtd', grad_qkv.reshape(slots, 3, N_TENSOR, width).astype(f32), qkv_weight.reshape(D, 3, N_TENSOR, width).astype(f32))
    grad_a1 = lax.optimization_barrier(jnp.sum(parts.astype(bf16).astype(f32), axis=0))
    grad_ln1_gain = lax.optimization_barrier(jnp.sum(grad_a1 * n1, axis=0))
    grad_ln1_shift = lax.optimization_barrier(jnp.sum(grad_a1, axis=0))
    grad_tokens = grad_h1 + norm_back(grad_a1, ln1_gain.astype(f32), n1, r1)
    grads = (grad_ln1_gain, grad_ln1_shift, grad_qkv_weight, grad_qkv_bias, grad_out_weight, grad_out_bias, grad_ln2_gain, grad_ln2_shift, grad_up_weight, grad_up_bias, grad_down_weight, grad_down_bias)
    return (output, grad_tokens, grads)

def reference(tokens, slot_seq, seq_len, ln1_gain, ln1_shift, qkv_weight, qkv_bias, out_weight, out_bias, ln2_gain, ln2_shift, up_weight, up_bias, down_weight, down_bias, cotangent):
    group_list = TOKENS // CAP
    params = (ln1_gain, ln1_shift, qkv_weight, qkv_bias, out_weight, out_bias, ln2_gain, ln2_shift, up_weight, up_bias, down_weight, down_bias)
    init = tuple((jnp.zeros(p.shape, jnp.float32) for p in params))
    scanned = (tokens.reshape(group_list, CAP, D), cotangent.reshape(group_list, CAP, D), slot_seq.reshape(group_list, CAP), seq_len.reshape(group_list, CAP // BLOCK))

    def step(carry, inputs):
        output, grad_tokens, grads = group_pass(params, inputs[0], inputs[1], inputs[2], inputs[3])
        return (tuple((c + g for c, g in zip(carry, grads))), (output, grad_tokens))
    totals, (outputs, grad_rows) = lax.scan(step, init, scanned)
    return (outputs.reshape(TOKENS, D), grad_rows.reshape(TOKENS, D), totals[0], totals[1], totals[2], totals[3], totals[4], totals[5], totals[6], totals[7], totals[8], totals[9], totals[10], totals[11])
```

```python
import functools

import jax
import jax.numpy as jnp
from jax import lax
from jax.experimental import pallas as pl
from jax.experimental.pallas import tpu as pltpu
from jax.sharding import PartitionSpec as P

HD = 64


epsilon = 1e-05
masked_fill = -1e30
gelu_root = 0.7978845608028654
gelu_cubic = 0.044715


def layer_norm(hidden, gain, shift):
    center = hidden - jnp.mean(hidden, axis=-1, keepdims=True)
    inverse = lax.rsqrt(jnp.mean(center * center, axis=-1, keepdims=True) + epsilon)
    normed = center * inverse
    return (normed * gain + shift, normed, inverse)


def norm_back(upstream, gain, normed, inverse):
    scaled = upstream * gain
    return inverse * (
        scaled
        - jnp.mean(scaled, axis=-1, keepdims=True)
        - normed * jnp.mean(scaled * normed, axis=-1, keepdims=True)
    )


def gelu_value(inputs):
    tangent = jnp.tanh(gelu_root * (inputs + gelu_cubic * inputs * inputs * inputs))
    return 0.5 * inputs * (1.0 + tangent)


def gelu_slope(inputs):
    tangent = jnp.tanh(gelu_root * (inputs + gelu_cubic * inputs * inputs * inputs))
    return 0.5 * (1.0 + tangent) + 0.5 * inputs * (1.0 - tangent * tangent) * gelu_root * (
        1.0 + 3.0 * gelu_cubic * inputs * inputs
    )


def live_slots(slot_seq, seq_len):
    numbers = seq_len.shape[0]
    onehot = (slot_seq[:, None] == jnp.arange(numbers, dtype=jnp.int32)[None, :]).astype(jnp.int32)
    counts = jnp.sum(onehot, axis=0, dtype=jnp.int32)
    first_slot = jnp.cumsum(counts, dtype=jnp.int32) - counts
    run_start = jnp.sum(onehot * first_slot[None, :], axis=1, dtype=jnp.int32)
    run_length = jnp.sum(onehot * seq_len[None, :], axis=1, dtype=jnp.int32)
    places = jnp.arange(slot_seq.shape[0], dtype=jnp.int32) - run_start
    return places < run_length


LANES = 128
NT = (((1,), (1,)), ((), ()))
TN = (((0,), (0,)), ((), ()))
f32 = jnp.float32
bf16 = jnp.bfloat16


def half_mask(half):
    lane = lax.broadcasted_iota(jnp.int32, (1, LANES), 1)
    return (lane >= HD) == (half == 1)


def block_allowed(seq_col_ref, key_row_ref, first, rows, width):
    query_index = first + lax.broadcasted_iota(jnp.int32, (rows, width), 0)
    key_index = lax.broadcasted_iota(jnp.int32, (rows, width), 1)
    same = seq_col_ref[first : first + rows, :] == key_row_ref[:, :width]
    return same & (key_index <= query_index)


def attention_kernel(rows, seq_col_ref, key_row_ref, q_ref, k_ref, v_ref, o_ref, lse_ref):
    slots = q_ref.shape[0]
    value_sum = jnp.sum(v_ref[...].astype(f32), axis=0, keepdims=True)
    for first in range(0, slots, rows):
        width = first + rows
        allowed = block_allowed(seq_col_ref, key_row_ref, first, rows, width)
        out = jnp.zeros((rows, LANES), f32)
        tops = []
        for half in range(2):
            mask = half_mask(half)
            query = jnp.where(mask, q_ref[first:width, :], 0)
            scores = lax.dot_general(
                query, k_ref[:width, :], NT, preferred_element_type=f32
            ) * HD ** (-0.5)
            scores = jnp.where(allowed, scores, masked_fill)
            top = jnp.max(scores, axis=-1, keepdims=True)
            shifted = jnp.exp(scores - top)
            total = jnp.sum(shifted, axis=-1, keepdims=True)
            log_total = top + jnp.log(total)
            probs = (shifted * (1.0 / total)).astype(bf16)
            value = jnp.where(mask, v_ref[:width, :], 0)
            part = jnp.dot(probs, value, preferred_element_type=f32)
            part = jnp.where(top < 0.1 * masked_fill, jnp.where(mask, value_sum, 0.0), part)
            out = out + part
            lse_ref[0, first:width, half : half + 1] = log_total
        o_ref[first:width, :] = out.astype(bf16)


def attention(qkv, seq_col, key_row, pairs):
    slots = qkv.shape[0]
    rows = min(256, slots)
    column = lambda part: pl.BlockSpec((slots, LANES), lambda i: (0, part * pairs + i))
    return pl.pallas_call(
        functools.partial(attention_kernel, rows),
        grid=(pairs,),
        in_specs=[
            pl.BlockSpec((slots, 1), lambda i: (0, 0)),
            pl.BlockSpec((1, slots), lambda i: (0, 0)),
            column(0),
            column(1),
            column(2),
        ],
        out_specs=[
            pl.BlockSpec((slots, LANES), lambda i: (0, i)),
            pl.BlockSpec((1, slots, 2), lambda i: (i, 0, 0)),
        ],
        out_shape=[
            jax.ShapeDtypeStruct((slots, pairs * LANES), bf16),
            jax.ShapeDtypeStruct((pairs, slots, 2), f32),
        ],
        compiler_params=pltpu.CompilerParams(vmem_limit_bytes=40 * 1024 * 1024),
        cost_estimate=pl.CostEstimate(
            flops=pairs * slots * slots * 512,
            bytes_accessed=pairs * slots * LANES * 12,
            transcendentals=pairs * slots * slots,
        ),
        name="attention",
    )(seq_col, key_row, qkv, qkv, qkv)


def attention_back_kernel(
    rows,
    seq_col_ref,
    key_row_ref,
    q_ref,
    k_ref,
    v_ref,
    o_ref,
    lse_ref,
    do_ref,
    dq_ref,
    dk_ref,
    dv_ref,
    bias_ref,
    dk_sum,
    dv_sum,
):
    slots = q_ref.shape[0]
    dk_sum[...] = jnp.zeros_like(dk_sum)
    dv_sum[...] = jnp.zeros_like(dv_sum)
    dq_total = jnp.zeros((1, LANES), f32)
    for first in range(0, slots, rows):
        width = first + rows
        allowed = block_allowed(seq_col_ref, key_row_ref, first, rows, width)
        product = do_ref[first:width, :].astype(f32) * o_ref[first:width, :].astype(f32)
        dq = jnp.zeros((rows, LANES), f32)
        for half in range(2):
            mask = half_mask(half)
            query = jnp.where(mask, q_ref[first:width, :], 0)
            key = jnp.where(mask, k_ref[:width, :], 0)
            upstream = jnp.where(mask, do_ref[first:width, :], 0)
            delta = jnp.sum(jnp.where(mask, product, 0.0), axis=-1, keepdims=True)
            scores = lax.dot_general(query, key, NT, preferred_element_type=f32) * HD ** (-0.5)
            scores = jnp.where(allowed, scores, masked_fill)
            probs = jnp.exp(scores - lse_ref[0, first:width, half : half + 1])
            grad_probs = lax.dot_general(
                upstream, v_ref[:width, :], NT, preferred_element_type=f32
            )
            grad_scores = (probs * ((grad_probs - delta) * HD ** (-0.5))).astype(bf16)
            dq = dq + jnp.dot(grad_scores, key, preferred_element_type=f32)
            dk_sum[:width, :] += lax.dot_general(
                grad_scores, query, TN, preferred_element_type=f32
            )
            dv_sum[:width, :] += lax.dot_general(
                probs.astype(bf16), upstream, TN, preferred_element_type=f32
            )
        dq_ref[first:width, :] = dq.astype(bf16)
        dq_total = dq_total + jnp.sum(dq, axis=0, keepdims=True)
    dk_ref[...] = dk_sum[...].astype(bf16)
    dv_ref[...] = dv_sum[...].astype(bf16)
    bias_ref[0:1, :] = dq_total
    bias_ref[1:2, :] = jnp.sum(dv_sum[...], axis=0, keepdims=True)


def attention_back(qkv, seq_col, key_row, heads, lse, grad_heads, pairs):
    slots = qkv.shape[0]
    rows = min(256, slots)
    column = lambda part: pl.BlockSpec((slots, LANES), lambda i: (0, part * pairs + i))
    return pl.pallas_call(
        functools.partial(attention_back_kernel, rows),
        grid=(pairs,),
        in_specs=[
            pl.BlockSpec((slots, 1), lambda i: (0, 0)),
            pl.BlockSpec((1, slots), lambda i: (0, 0)),
            column(0),
            column(1),
            column(2),
            column(0),
            pl.BlockSpec((1, slots, 2), lambda i: (i, 0, 0)),
            column(0),
        ],
        out_specs=[column(0), column(0), column(0), pl.BlockSpec((2, LANES), lambda i: (0, i))],
        out_shape=[jax.ShapeDtypeStruct((slots, pairs * LANES), bf16)] * 3
        + [jax.ShapeDtypeStruct((2, pairs * LANES), f32)],
        scratch_shapes=[pltpu.VMEM((slots, LANES), f32), pltpu.VMEM((slots, LANES), f32)],
        compiler_params=pltpu.CompilerParams(vmem_limit_bytes=40 * 1024 * 1024),
        cost_estimate=pl.CostEstimate(
            flops=pairs * slots * slots * 1280,
            bytes_accessed=pairs * slots * LANES * 20,
            transcendentals=pairs * slots * slots,
        ),
        name="attention_back",
    )(seq_col, key_row, qkv, qkv, qkv, heads, lse, grad_heads)


def swap(block):
    return lax.ppermute(block, "tensor", [(0, 1), (1, 0)])


def gather_rows(block):
    if lax.axis_size("tensor") != 2:
        return lax.all_gather(block, "tensor", axis=0, tiled=True)
    other = swap(block)
    return jnp.where(
        lax.axis_index("tensor") == 0,
        jnp.concatenate([block, other], axis=0),
        jnp.concatenate([other, block], axis=0),
    )


def own_sum(left, right, own_rows):
    product = lambda rows: lax.dot_general(rows, right, NT, preferred_element_type=f32).astype(bf16)
    if lax.axis_size("tensor") != 2:
        total = product(left)
        return (
            lax.psum_scatter(total, "tensor", scatter_dimension=0, tiled=True).astype(f32),
            total,
        )
    me = lax.axis_index("tensor")
    send = product(lax.dynamic_slice_in_dim(left, (1 - me) * own_rows, own_rows))
    arrived = swap(send)
    keep = product(lax.dynamic_slice_in_dim(left, me * own_rows, own_rows))
    return keep.astype(f32) + arrived.astype(f32), (send, keep)


def as_columns(vector, rows):
    flat = vector.reshape(-1)
    columns = -(-flat.shape[0] // rows)
    return jnp.pad(flat, (0, columns * rows - flat.shape[0])).reshape(rows, columns)


def pad_columns(array):
    return jnp.pad(array, ((0, 0), (0, -array.shape[1] % LANES)))


def scatter_groups(array):
    return lax.psum_scatter(array, "dp", scatter_dimension=0, tiled=True).astype(f32)


def local(
    tokens,
    slot_seq,
    seq_len,
    ln1_gain,
    ln1_shift,
    qkv_weight,
    qkv_bias,
    out_weight,
    out_bias,
    ln2_gain,
    ln2_shift,
    up_weight,
    up_bias,
    down_weight,
    down_bias,
    cotangent,
):
    own_rows, width = tokens.shape
    slots = slot_seq.shape[0]
    shard = ln1_gain.shape[0]
    groups = lax.axis_size("dp")
    me = lax.axis_index("tensor")
    here = qkv_weight.shape[2]
    hidden = up_weight.shape[1]
    heads_here = here // HD
    pairs = here // LANES

    vectors = jnp.stack([ln1_gain, ln1_shift, out_bias, ln2_gain, ln2_shift, down_bias], axis=1)
    up_bias_columns = as_columns(up_bias, shard)
    qkv_bias_columns = as_columns(qkv_bias, shard)
    small = pad_columns(
        jnp.concatenate([vectors, up_bias_columns, qkv_bias_columns], axis=1)
    )
    first_piece = jnp.concatenate(
        [qkv_weight.reshape(shard, 3 * here), out_weight.T, small], axis=1
    )
    first_all = lax.all_gather(first_piece, "dp", axis=0, tiled=True)
    second_all = lax.all_gather(
        jnp.concatenate([up_weight, down_weight.T], axis=1), "dp", axis=0, tiled=True
    )
    w_qkv = first_all[:, : 3 * here]
    w_out_t = first_all[:, 3 * here : 4 * here]
    w_up = second_all[:, :hidden]
    w_down_t = second_all[:, hidden:]
    small_all = first_all[:, 4 * here :].astype(f32)
    gain_one, shift_one, bias_out, gain_two, shift_two, bias_down = (
        small_all[:, i] for i in range(6)
    )

    def unpack(start, columns, shape, axis):
        flat = small_all[:, start : start + columns].reshape(groups, shard * columns)
        count = 1
        for size in shape:
            count *= size
        parts = flat[:, :count].reshape((groups,) + shape)
        parts = jnp.moveaxis(parts, 0, axis)
        return parts.reshape(shape[:axis] + (groups * shape[axis],) + shape[axis + 1 :])

    up_columns = up_bias_columns.shape[1]
    bias_up = unpack(6, up_columns, up_bias.shape, 1).reshape(-1)
    bias_rows = unpack(6 + up_columns, qkv_bias_columns.shape[1], qkv_bias.shape, 2).reshape(
        2, here
    )
    bias_qkv = jnp.concatenate([bias_rows[0], jnp.zeros_like(bias_rows[0]), bias_rows[1]])

    live = live_slots(slot_seq, seq_len)
    own_live = lax.dynamic_slice_in_dim(live, me * own_rows, own_rows)
    seq_col = slot_seq[:, None]
    key_row = jnp.where(live, slot_seq, -1)[None, :]

    tokens_all = gather_rows(tokens)
    cotangent_all = gather_rows(cotangent)
    grad_h2_all = jnp.where(live[:, None], cotangent_all, jnp.zeros_like(cotangent_all))

    a1_full, normed_one_all, _ = layer_norm(tokens_all.astype(f32), gain_one, shift_one)
    a1_all = a1_full.astype(bf16)
    qkv = (jnp.dot(a1_all, w_qkv, preferred_element_type=f32) + bias_qkv).astype(bf16)
    heads, lse = attention(qkv, seq_col, key_row, pairs)
    attn, _ = own_sum(heads, w_out_t, own_rows)
    inputs = tokens.astype(f32)
    hidden_one = inputs + attn + bias_out
    a2_full, normed_two, inverse_two = layer_norm(hidden_one, gain_two, shift_two)
    a2_all = gather_rows(a2_full.astype(bf16))
    pre = jnp.dot(a2_all, w_up, preferred_element_type=f32) + bias_up
    act = gelu_value(pre).astype(bf16)
    grad_down_weight_t = lax.dot_general(grad_h2_all, act, TN, preferred_element_type=f32)
    grad_pre = jnp.dot(grad_h2_all, w_down_t, preferred_element_type=f32) * gelu_slope(pre)
    grad_up_bias = jnp.sum(grad_pre, axis=0)
    grad_pre_b = grad_pre.astype(bf16)
    grad_a2, _ = own_sum(grad_pre_b, w_up, own_rows)
    grad_up_weight = lax.dot_general(a2_all, grad_pre_b, TN, preferred_element_type=f32)
    second_sum = scatter_groups(
        jnp.concatenate([grad_up_weight.astype(bf16), grad_down_weight_t.astype(bf16)], axis=1)
    )

    mlp, _ = own_sum(act, w_down_t, own_rows)
    output = jnp.where(own_live[:, None], hidden_one + mlp + bias_down, 0.0)

    grad_h2 = jnp.where(own_live[:, None], cotangent.astype(f32), 0.0)
    grad_down_bias = jnp.sum(grad_h2, axis=0)
    grad_ln2_gain = jnp.sum(grad_a2 * normed_two, axis=0)
    grad_ln2_shift = jnp.sum(grad_a2, axis=0)
    grad_h1 = grad_h2 + norm_back(grad_a2, gain_two, normed_two, inverse_two)
    grad_out_bias = jnp.sum(grad_h1, axis=0)
    grad_h1_all = gather_rows(grad_h1.astype(bf16))
    grad_heads = jnp.dot(grad_h1_all, w_out_t, preferred_element_type=f32).astype(bf16)
    grad_out_weight_t = lax.dot_general(grad_h1_all, heads, TN, preferred_element_type=f32)
    dq, dk, dv, grad_qkv_bias = attention_back(
        qkv, seq_col, key_row, heads, lse, grad_heads, pairs
    )
    grad_qkv = jnp.concatenate([dq, dk, dv], axis=1)
    grad_a1, parts = own_sum(grad_qkv, w_qkv, own_rows)
    if lax.axis_size("tensor") == 2:
        send, keep = (part.astype(f32) for part in parts)
        rows_at = lambda place: lax.dynamic_slice_in_dim(normed_one_all, place * own_rows, own_rows)
        grad_ln1_gain = jnp.sum(send * rows_at(1 - me) + keep * rows_at(me), axis=0)
        grad_ln1_shift = jnp.sum(send + keep, axis=0)
    else:
        grad_ln1_gain = jnp.sum(parts.astype(f32) * normed_one_all, axis=0)
        grad_ln1_shift = jnp.sum(parts.astype(f32), axis=0)
    grad_qkv_weight = lax.dot_general(a1_all, grad_qkv, TN, preferred_element_type=f32)

    def pack(gradient, shape, axis):
        parts = gradient.reshape(shape[:axis] + (groups, shape[axis]) + shape[axis + 1 :])
        flat = jnp.moveaxis(parts, axis, 0).reshape(groups, -1)
        columns = -(-flat.shape[1] // shard)
        flat = jnp.pad(flat, ((0, 0), (0, columns * shard - flat.shape[1])))
        return flat.reshape(groups * shard, columns)

    grad_vectors = jnp.stack(
        [
            grad_ln1_gain,
            grad_ln1_shift,
            grad_out_bias,
            grad_ln2_gain,
            grad_ln2_shift,
            grad_down_bias,
        ],
        axis=1,
    )
    grad_small = pad_columns(
        jnp.concatenate(
            [
                grad_vectors,
                pack(grad_up_bias, up_bias.shape, 1),
                pack(grad_qkv_bias, qkv_bias.shape, 2),
            ],
            axis=1,
        )
    )
    first_sum = scatter_groups(
        jnp.concatenate(
            [
                grad_qkv_weight.astype(bf16),
                grad_out_weight_t.astype(bf16),
                grad_small.astype(bf16),
            ],
            axis=1,
        )
    )
    normed_one, inverse_one = layer_norm(inputs, gain_one, shift_one)[1:]
    grad_tokens = grad_h1 + norm_back(grad_a1, gain_one, normed_one, inverse_one)

    small_sum = first_sum[:, 4 * here :]
    vector_sum = small_sum[:, :6].T
    if lax.axis_size("tensor") == 2:
        vector_sum = vector_sum + swap(vector_sum)
    else:
        vector_sum = lax.psum(vector_sum, "tensor")
    up_bias_sum = small_sum[:, 6 : 6 + up_columns].reshape(-1)[: up_bias.size]
    qkv_columns = qkv_bias_columns.shape[1]
    qkv_bias_sum = small_sum[:, 6 + up_columns : 6 + up_columns + qkv_columns].reshape(-1)
    return (
        output,
        grad_tokens,
        vector_sum[0],
        vector_sum[1],
        first_sum[:, : 3 * here].reshape(shard, 3, here),
        qkv_bias_sum[: qkv_bias.size].reshape(qkv_bias.shape),
        first_sum[:, 3 * here : 4 * here].T,
        vector_sum[2],
        vector_sum[3],
        vector_sum[4],
        second_sum[:, :hidden],
        up_bias_sum.reshape(up_bias.shape),
        second_sum[:, hidden:].T,
        vector_sum[5],
    )


def solution(mesh):
    placed = (
        P(("dp", "tensor"), None),
        P("dp"),
        P("dp"),
        P("dp"),
        P("dp"),
        P("dp", None, "tensor"),
        P(None, "tensor", "dp"),
        P("tensor", "dp"),
        P("dp"),
        P("dp"),
        P("dp"),
        P("dp", "tensor"),
        P("tensor", "dp"),
        P("tensor", "dp"),
        P("dp"),
        P(("dp", "tensor"), None),
    )
    return jax.shard_map(
        local,
        mesh=mesh,
        in_specs=placed,
        out_specs=(
            P(("dp", "tensor"), None),
            P(("dp", "tensor"), None),
            P("dp"),
            P("dp"),
            P("dp", None, "tensor"),
            P(None, "tensor", "dp"),
            P("tensor", "dp"),
            P("dp"),
            P("dp"),
            P("dp"),
            P("dp", "tensor"),
            P("tensor", "dp"),
            P("tensor", "dp"),
            P("dp"),
        ),
        check_vma=False,
    )
```

```python
import functools

import jax
import jax.numpy as jnp
from jax import lax
from jax.experimental import pallas as pl
from jax.experimental.pallas import tpu as pltpu
from jax.sharding import PartitionSpec as P

HD = 64


epsilon = 1e-05
masked_fill = -1e30
gelu_root = 0.7978845608028654
gelu_cubic = 0.044715


def layer_norm(hidden, gain, shift):
    center = hidden - jnp.mean(hidden, axis=-1, keepdims=True)
    inverse = lax.rsqrt(jnp.mean(center * center, axis=-1, keepdims=True) + epsilon)
    normed = center * inverse
    return (normed * gain + shift, normed, inverse)


def norm_back(upstream, gain, normed, inverse):
    scaled = upstream * gain
    return inverse * (
        scaled
        - jnp.mean(scaled, axis=-1, keepdims=True)
        - normed * jnp.mean(scaled * normed, axis=-1, keepdims=True)
    )


def gelu_value(inputs):
    tangent = jnp.tanh(gelu_root * (inputs + gelu_cubic * inputs * inputs * inputs))
    return 0.5 * inputs * (1.0 + tangent)


def gelu_slope(inputs):
    tangent = jnp.tanh(gelu_root * (inputs + gelu_cubic * inputs * inputs * inputs))
    return 0.5 * (1.0 + tangent) + 0.5 * inputs * (1.0 - tangent * tangent) * gelu_root * (
        1.0 + 3.0 * gelu_cubic * inputs * inputs
    )


def live_slots(slot_seq, seq_len):
    numbers = seq_len.shape[0]
    onehot = (slot_seq[:, None] == jnp.arange(numbers, dtype=jnp.int32)[None, :]).astype(jnp.int32)
    counts = jnp.sum(onehot, axis=0, dtype=jnp.int32)
    first_slot = jnp.cumsum(counts, dtype=jnp.int32) - counts
    run_start = jnp.sum(onehot * first_slot[None, :], axis=1, dtype=jnp.int32)
    run_length = jnp.sum(onehot * seq_len[None, :], axis=1, dtype=jnp.int32)
    places = jnp.arange(slot_seq.shape[0], dtype=jnp.int32) - run_start
    return places < run_length


LANES = 128
NT = (((1,), (1,)), ((), ()))
TN = (((0,), (0,)), ((), ()))
f32 = jnp.float32
bf16 = jnp.bfloat16


def half_mask(half):
    lane = lax.broadcasted_iota(jnp.int32, (1, LANES), 1)
    return (lane >= HD) == (half == 1)


def block_allowed(seq_col_ref, key_row_ref, first, rows, width):
    query_index = first + lax.broadcasted_iota(jnp.int32, (rows, width), 0)
    key_index = lax.broadcasted_iota(jnp.int32, (rows, width), 1)
    same = seq_col_ref[first : first + rows, :] == key_row_ref[:, :width]
    return same & (key_index <= query_index)


def attention_kernel(rows, seq_col_ref, key_row_ref, q_ref, k_ref, v_ref, o_ref, lse_ref):
    slots = q_ref.shape[0]
    value_sum = jnp.sum(v_ref[...].astype(f32), axis=0, keepdims=True)
    for first in range(0, slots, rows):
        width = first + rows
        allowed = block_allowed(seq_col_ref, key_row_ref, first, rows, width)
        out = jnp.zeros((rows, LANES), f32)
        tops = []
        for half in range(2):
            mask = half_mask(half)
            query = jnp.where(mask, q_ref[first:width, :], 0)
            scores = lax.dot_general(
                query, k_ref[:width, :], NT, preferred_element_type=f32
            ) * HD ** (-0.5)
            scores = jnp.where(allowed, scores, masked_fill)
            top = jnp.max(scores, axis=-1, keepdims=True)
            shifted = jnp.exp(scores - top)
            total = jnp.sum(shifted, axis=-1, keepdims=True)
            log_total = top + jnp.log(total)
            probs = (shifted * (1.0 / total)).astype(bf16)
            value = jnp.where(mask, v_ref[:width, :], 0)
            part = jnp.dot(probs, value, preferred_element_type=f32)
            part = jnp.where(top < 0.1 * masked_fill, jnp.where(mask, value_sum, 0.0), part)
            out = out + part
            lse_ref[0, first:width, half : half + 1] = log_total
        o_ref[first:width, :] = out.astype(bf16)


def attention(qkv, seq_col, key_row, pairs):
    slots = qkv.shape[0]
    rows = min(256, slots)
    column = lambda part: pl.BlockSpec((slots, LANES), lambda i: (0, part * pairs + i))
    return pl.pallas_call(
        functools.partial(attention_kernel, rows),
        grid=(pairs,),
        in_specs=[
            pl.BlockSpec((slots, 1), lambda i: (0, 0)),
            pl.BlockSpec((1, slots), lambda i: (0, 0)),
            column(0),
            column(1),
            column(2),
        ],
        out_specs=[
            pl.BlockSpec((slots, LANES), lambda i: (0, i)),
            pl.BlockSpec((1, slots, 2), lambda i: (i, 0, 0)),
        ],
        out_shape=[
            jax.ShapeDtypeStruct((slots, pairs * LANES), bf16),
            jax.ShapeDtypeStruct((pairs, slots, 2), f32),
        ],
        compiler_params=pltpu.CompilerParams(vmem_limit_bytes=40 * 1024 * 1024),
        cost_estimate=pl.CostEstimate(
            flops=pairs * slots * slots * 512,
            bytes_accessed=pairs * slots * LANES * 12,
            transcendentals=pairs * slots * slots,
        ),
        name="attention",
    )(seq_col, key_row, qkv, qkv, qkv)


def attention_back_kernel(
    rows,
    seq_col_ref,
    key_row_ref,
    q_ref,
    k_ref,
    v_ref,
    o_ref,
    lse_ref,
    do_ref,
    dq_ref,
    dk_ref,
    dv_ref,
    bias_ref,
    dk_sum,
    dv_sum,
):
    slots = q_ref.shape[0]
    dk_sum[...] = jnp.zeros_like(dk_sum)
    dv_sum[...] = jnp.zeros_like(dv_sum)
    dq_total = jnp.zeros((1, LANES), f32)
    for first in range(0, slots, rows):
        width = first + rows
        allowed = block_allowed(seq_col_ref, key_row_ref, first, rows, width)
        product = do_ref[first:width, :].astype(f32) * o_ref[first:width, :].astype(f32)
        dq = jnp.zeros((rows, LANES), f32)
        for half in range(2):
            mask = half_mask(half)
            query = jnp.where(mask, q_ref[first:width, :], 0)
            key = jnp.where(mask, k_ref[:width, :], 0)
            upstream = jnp.where(mask, do_ref[first:width, :], 0)
            delta = jnp.sum(jnp.where(mask, product, 0.0), axis=-1, keepdims=True)
            scores = lax.dot_general(query, key, NT, preferred_element_type=f32) * HD ** (-0.5)
            scores = jnp.where(allowed, scores, masked_fill)
            probs = jnp.exp(scores - lse_ref[0, first:width, half : half + 1])
            grad_probs = lax.dot_general(
                upstream, v_ref[:width, :], NT, preferred_element_type=f32
            )
            grad_scores = (probs * ((grad_probs - delta) * HD ** (-0.5))).astype(bf16)
            dq = dq + jnp.dot(grad_scores, key, preferred_element_type=f32)
            dk_sum[:width, :] += lax.dot_general(
                grad_scores, query, TN, preferred_element_type=f32
            )
            dv_sum[:width, :] += lax.dot_general(
                probs.astype(bf16), upstream, TN, preferred_element_type=f32
            )
        dq_ref[first:width, :] = dq.astype(bf16)
        dq_total = dq_total + jnp.sum(dq, axis=0, keepdims=True)
    dk_ref[...] = dk_sum[...].astype(bf16)
    dv_ref[...] = dv_sum[...].astype(bf16)
    bias_ref[0:1, :] = dq_total
    bias_ref[1:2, :] = jnp.sum(dv_sum[...], axis=0, keepdims=True)


def attention_back(qkv, seq_col, key_row, heads, lse, grad_heads, pairs):
    slots = qkv.shape[0]
    rows = min(256, slots)
    column = lambda part: pl.BlockSpec((slots, LANES), lambda i: (0, part * pairs + i))
    return pl.pallas_call(
        functools.partial(attention_back_kernel, rows),
        grid=(pairs,),
        in_specs=[
            pl.BlockSpec((slots, 1), lambda i: (0, 0)),
            pl.BlockSpec((1, slots), lambda i: (0, 0)),
            column(0),
            column(1),
            column(2),
            column(0),
            pl.BlockSpec((1, slots, 2), lambda i: (i, 0, 0)),
            column(0),
        ],
        out_specs=[column(0), column(0), column(0), pl.BlockSpec((2, LANES), lambda i: (0, i))],
        out_shape=[jax.ShapeDtypeStruct((slots, pairs * LANES), bf16)] * 3
        + [jax.ShapeDtypeStruct((2, pairs * LANES), f32)],
        scratch_shapes=[pltpu.VMEM((slots, LANES), f32), pltpu.VMEM((slots, LANES), f32)],
        compiler_params=pltpu.CompilerParams(vmem_limit_bytes=40 * 1024 * 1024),
        cost_estimate=pl.CostEstimate(
            flops=pairs * slots * slots * 1280,
            bytes_accessed=pairs * slots * LANES * 20,
            transcendentals=pairs * slots * slots,
        ),
        name="attention_back",
    )(seq_col, key_row, qkv, qkv, qkv, heads, lse, grad_heads)


def swap(block):
    return lax.ppermute(block, "tensor", [(0, 1), (1, 0)])


def gather_rows(block):
    if lax.axis_size("tensor") != 2:
        return lax.all_gather(block, "tensor", axis=0, tiled=True)
    other = swap(block)
    return jnp.where(
        lax.axis_index("tensor") == 0,
        jnp.concatenate([block, other], axis=0),
        jnp.concatenate([other, block], axis=0),
    )


def own_sum(left, right, own_rows):
    product = lambda rows: lax.dot_general(rows, right, NT, preferred_element_type=f32).astype(bf16)
    if lax.axis_size("tensor") != 2:
        total = product(left)
        return (
            lax.psum_scatter(total, "tensor", scatter_dimension=0, tiled=True).astype(f32),
            total,
        )
    me = lax.axis_index("tensor")
    send = product(lax.dynamic_slice_in_dim(left, (1 - me) * own_rows, own_rows))
    arrived = swap(send)
    keep = product(lax.dynamic_slice_in_dim(left, me * own_rows, own_rows))
    return keep.astype(f32) + arrived.astype(f32), (send, keep)


def row_blocks(block):
    if lax.axis_size("tensor") != 2:
        return [lax.all_gather(block, "tensor", axis=0, tiled=True)]
    return [block, swap(block)]


def block_sum(blocks, right):
    product = lambda rows: lax.dot_general(rows, right, NT, preferred_element_type=f32).astype(bf16)
    if len(blocks) == 1:
        total = lax.psum_scatter(product(blocks[0]), "tensor", scatter_dimension=0, tiled=True)
        return total, jnp.zeros_like(total)
    arrived = swap(product(blocks[1]))
    return product(blocks[0]), arrived


def as_columns(vector, rows):
    flat = vector.reshape(-1)
    columns = -(-flat.shape[0] // rows)
    return jnp.pad(flat, (0, columns * rows - flat.shape[0])).reshape(rows, columns)


def pad_columns(array):
    return jnp.pad(array, ((0, 0), (0, -array.shape[1] % LANES)))


def scatter_groups(array):
    return lax.psum_scatter(array, "dp", scatter_dimension=0, tiled=True).astype(f32)


def halving_sum(array):
    devices = lax.axis_size("dp")
    if devices & (devices - 1):
        return scatter_groups(array)
    place = lax.axis_index("dp")
    rows, columns = array.shape[0] // devices, array.shape[1]
    step = 1
    while step < devices:
        halves = array.reshape(devices // (2 * step), 2, rows, columns)
        bit = (place // step) % 2
        half = lambda which: lax.dynamic_index_in_dim(halves, which, 1, keepdims=False)
        arrived = lax.ppermute(half(1 - bit), "dp", [(i, i ^ step) for i in range(devices)])
        total = half(bit).astype(f32) + arrived.astype(f32)
        step *= 2
        array = total.astype(bf16)
    return total.reshape(rows, columns)


def local(
    tokens,
    slot_seq,
    seq_len,
    ln1_gain,
    ln1_shift,
    qkv_weight,
    qkv_bias,
    out_weight,
    out_bias,
    ln2_gain,
    ln2_shift,
    up_weight,
    up_bias,
    down_weight,
    down_bias,
    cotangent,
):
    own_rows, width = tokens.shape
    slots = slot_seq.shape[0]
    shard = ln1_gain.shape[0]
    groups = lax.axis_size("dp")
    me = lax.axis_index("tensor")
    here = qkv_weight.shape[2]
    hidden = up_weight.shape[1]
    heads_here = here // HD
    pairs = here // LANES

    vectors = jnp.stack([ln1_gain, ln1_shift, out_bias, ln2_gain, ln2_shift, down_bias], axis=1)
    up_bias_columns = as_columns(up_bias, shard)
    qkv_bias_columns = as_columns(qkv_bias, shard)
    small = pad_columns(
        jnp.concatenate([vectors, up_bias_columns, qkv_bias_columns], axis=1)
    )
    first_piece = jnp.concatenate(
        [qkv_weight.reshape(shard, 3 * here), out_weight.T, small], axis=1
    )
    first_all = lax.all_gather(first_piece, "dp", axis=0, tiled=True)
    second_all = lax.all_gather(
        jnp.concatenate([up_weight, down_weight.T], axis=1), "dp", axis=0, tiled=True
    )
    w_qkv = first_all[:, : 3 * here]
    w_out_t = first_all[:, 3 * here : 4 * here]
    w_up = second_all[:, :hidden]
    w_down_t = second_all[:, hidden:]
    small_all = first_all[:, 4 * here :].astype(f32)
    gain_one, shift_one, bias_out, gain_two, shift_two, bias_down = (
        small_all[:, i] for i in range(6)
    )

    def unpack(start, columns, shape, axis):
        flat = small_all[:, start : start + columns].reshape(groups, shard * columns)
        count = 1
        for size in shape:
            count *= size
        parts = flat[:, :count].reshape((groups,) + shape)
        parts = jnp.moveaxis(parts, 0, axis)
        return parts.reshape(shape[:axis] + (groups * shape[axis],) + shape[axis + 1 :])

    up_columns = up_bias_columns.shape[1]
    bias_up = unpack(6, up_columns, up_bias.shape, 1).reshape(-1)
    bias_rows = unpack(6 + up_columns, qkv_bias_columns.shape[1], qkv_bias.shape, 2).reshape(
        2, here
    )
    bias_qkv = jnp.concatenate([bias_rows[0], jnp.zeros_like(bias_rows[0]), bias_rows[1]])

    live = live_slots(slot_seq, seq_len)
    own_live = lax.dynamic_slice_in_dim(live, me * own_rows, own_rows)
    seq_col = slot_seq[:, None]
    key_row = jnp.where(live, slot_seq, -1)[None, :]

    tokens_all = gather_rows(tokens)
    tokens_all, cotangent = lax.optimization_barrier((tokens_all, cotangent))
    live_blocks = [live]
    if lax.axis_size("tensor") == 2:
        live_blocks = [
            own_live,
            lax.dynamic_slice_in_dim(live, (1 - me) * own_rows, own_rows),
        ]
    grad_h2_blocks = [
        jnp.where(here_live[:, None], block, jnp.zeros_like(block))
        for here_live, block in zip(live_blocks, row_blocks(cotangent))
    ]
    tokens_all, grad_h2_blocks = lax.optimization_barrier((tokens_all, grad_h2_blocks))
    grad_h2_all = jnp.concatenate(grad_h2_blocks, axis=0)

    a1_full, normed_one_all, _ = layer_norm(tokens_all.astype(f32), gain_one, shift_one)
    a1_all = a1_full.astype(bf16)
    qkv = (jnp.dot(a1_all, w_qkv, preferred_element_type=f32) + bias_qkv).astype(bf16)
    heads, lse = attention(qkv, seq_col, key_row, pairs)
    attn, _ = own_sum(heads, w_out_t, own_rows)
    inputs = tokens.astype(f32)
    hidden_one = inputs + attn + bias_out
    a2_full, normed_two, inverse_two = layer_norm(hidden_one, gain_two, shift_two)
    a2_blocks = row_blocks(a2_full.astype(bf16))
    act_blocks, grad_pre_blocks = [], []
    grad_up_bias = 0.0
    for index, (a2_block, grad_block) in enumerate(zip(a2_blocks, grad_h2_blocks)):
        pre = jnp.dot(a2_block, w_up, preferred_element_type=f32) + bias_up
        act_blocks.append(gelu_value(pre).astype(bf16))
        grad_pre = jnp.dot(grad_block, w_down_t, preferred_element_type=f32) * gelu_slope(pre)
        grad_up_bias = grad_up_bias + jnp.sum(grad_pre, axis=0)
        grad_pre_blocks.append(grad_pre.astype(bf16))
        if index + 1 < len(a2_blocks):
            act_blocks[0], grad_pre_blocks[0], grad_up_bias, a2_blocks[1] = (
                lax.optimization_barrier(
                    (act_blocks[0], grad_pre_blocks[0], grad_up_bias, a2_blocks[1])
                )
            )
    act = jnp.concatenate(act_blocks, axis=0)
    grad_pre_b = jnp.concatenate(grad_pre_blocks, axis=0)
    a2_all = jnp.concatenate(a2_blocks, axis=0)
    grad_a2_keep, grad_a2_arrived = block_sum(grad_pre_blocks, w_up)
    grad_down_weight_t = lax.dot_general(grad_h2_all, act, TN, preferred_element_type=f32)
    grad_up_weight = lax.dot_general(a2_all, grad_pre_b, TN, preferred_element_type=f32)
    second_piece = jnp.concatenate(
        [grad_up_weight.astype(bf16), grad_down_weight_t.astype(bf16)], axis=1
    )
    grad_a2_keep, grad_a2_arrived, second_piece = lax.optimization_barrier(
        (grad_a2_keep, grad_a2_arrived, second_piece)
    )
    second_sum = scatter_groups(second_piece)
    grad_a2 = grad_a2_keep.astype(f32) + grad_a2_arrived.astype(f32)

    grad_h2 = jnp.where(own_live[:, None], cotangent.astype(f32), 0.0)
    grad_down_bias = jnp.sum(grad_h2, axis=0)
    grad_ln2_gain = jnp.sum(grad_a2 * normed_two, axis=0)
    grad_ln2_shift = jnp.sum(grad_a2, axis=0)
    grad_h1 = grad_h2 + norm_back(grad_a2, gain_two, normed_two, inverse_two)
    grad_out_bias = jnp.sum(grad_h1, axis=0)
    grad_h1_all = gather_rows(grad_h1.astype(bf16))
    grad_h1_all, act_blocks = lax.optimization_barrier((grad_h1_all, act_blocks))
    mlp_keep, mlp_arrived = block_sum(act_blocks, w_down_t)
    grad_heads = jnp.dot(grad_h1_all, w_out_t, preferred_element_type=f32).astype(bf16)
    grad_out_weight_t = lax.dot_general(grad_h1_all, heads, TN, preferred_element_type=f32)
    dq, dk, dv, grad_qkv_bias = attention_back(
        qkv, seq_col, key_row, heads, lse, grad_heads, pairs
    )
    dq, dk, dv, mlp_keep, mlp_arrived = lax.optimization_barrier(
        (dq, dk, dv, mlp_keep, mlp_arrived)
    )
    mlp = mlp_keep.astype(f32) + mlp_arrived.astype(f32)
    output = jnp.where(own_live[:, None], hidden_one + mlp + bias_down, 0.0)
    grad_qkv = jnp.concatenate([dq, dk, dv], axis=1)
    grad_a1, parts = own_sum(grad_qkv, w_qkv, own_rows)
    if lax.axis_size("tensor") == 2:
        send, keep = (part.astype(f32) for part in parts)
        rows_at = lambda place: lax.dynamic_slice_in_dim(normed_one_all, place * own_rows, own_rows)
        grad_ln1_gain = jnp.sum(send * rows_at(1 - me) + keep * rows_at(me), axis=0)
        grad_ln1_shift = jnp.sum(send + keep, axis=0)
    else:
        grad_ln1_gain = jnp.sum(parts.astype(f32) * normed_one_all, axis=0)
        grad_ln1_shift = jnp.sum(parts.astype(f32), axis=0)
    grad_qkv_weight = lax.dot_general(a1_all, grad_qkv, TN, preferred_element_type=f32)

    def pack(gradient, shape, axis):
        parts = gradient.reshape(shape[:axis] + (groups, shape[axis]) + shape[axis + 1 :])
        flat = jnp.moveaxis(parts, axis, 0).reshape(groups, -1)
        columns = -(-flat.shape[1] // shard)
        flat = jnp.pad(flat, ((0, 0), (0, columns * shard - flat.shape[1])))
        return flat.reshape(groups * shard, columns)

    grad_vectors = jnp.stack(
        [
            grad_ln1_gain,
            grad_ln1_shift,
            grad_out_bias,
            grad_ln2_gain,
            grad_ln2_shift,
            grad_down_bias,
        ],
        axis=1,
    )
    grad_small = pad_columns(
        jnp.concatenate(
            [
                grad_vectors,
                pack(grad_up_bias, up_bias.shape, 1),
                pack(grad_qkv_bias, qkv_bias.shape, 2),
            ],
            axis=1,
        )
    )
    out_sum = halving_sum(grad_out_weight_t.astype(bf16))
    qkv_sum = halving_sum(grad_qkv_weight.astype(bf16))
    small_sum = halving_sum(grad_small.astype(bf16))
    normed_one, inverse_one = layer_norm(inputs, gain_one, shift_one)[1:]
    grad_tokens = grad_h1 + norm_back(grad_a1, gain_one, normed_one, inverse_one)

    vector_sum = small_sum[:, :6].T
    if lax.axis_size("tensor") == 2:
        vector_sum = vector_sum + swap(vector_sum)
    else:
        vector_sum = lax.psum(vector_sum, "tensor")
    up_bias_sum = small_sum[:, 6 : 6 + up_columns].reshape(-1)[: up_bias.size]
    qkv_columns = qkv_bias_columns.shape[1]
    qkv_bias_sum = small_sum[:, 6 + up_columns : 6 + up_columns + qkv_columns].reshape(-1)
    return (
        output,
        grad_tokens,
        vector_sum[0],
        vector_sum[1],
        qkv_sum.reshape(shard, 3, here),
        qkv_bias_sum[: qkv_bias.size].reshape(qkv_bias.shape),
        out_sum.T,
        vector_sum[2],
        vector_sum[3],
        vector_sum[4],
        second_sum[:, :hidden],
        up_bias_sum.reshape(up_bias.shape),
        second_sum[:, hidden:].T,
        vector_sum[5],
    )


def solution(mesh):
    placed = (
        P(("dp", "tensor"), None),
        P("dp"),
        P("dp"),
        P("dp"),
        P("dp"),
        P("dp", None, "tensor"),
        P(None, "tensor", "dp"),
        P("tensor", "dp"),
        P("dp"),
        P("dp"),
        P("dp"),
        P("dp", "tensor"),
        P("tensor", "dp"),
        P("tensor", "dp"),
        P("dp"),
        P(("dp", "tensor"), None),
    )
    return jax.shard_map(
        local,
        mesh=mesh,
        in_specs=placed,
        out_specs=(
            P(("dp", "tensor"), None),
            P(("dp", "tensor"), None),
            P("dp"),
            P("dp"),
            P("dp", None, "tensor"),
            P(None, "tensor", "dp"),
            P("tensor", "dp"),
            P("dp"),
            P("dp"),
            P("dp"),
            P("dp", "tensor"),
            P("tensor", "dp"),
            P("tensor", "dp"),
            P("dp"),
        ),
        check_vma=False,
    )
```
